128 devices in a mesh: rep: 8 (over x_lo, z), shard: 16 (over y, x_hi, core).
Axes of the slice: x: 4 (x_hi: 2, x_lo: 2; x = x_hi * 2 + x_lo), y: 4, z: 4, core: 2. Of those that a mesh axis runs over, the one named last changes fastest.
Arguments:
- tokens: bfloat16 [32768, 8192], P(('rep', 'shard')), may hold values from -6 to 6
- grad_values: bfloat16 [32768, 1024], P(('rep', 'shard')), may hold values from -6 to 6
- weights: bfloat16 [8, 4, 8192, 1024], P('rep', None, 'shard'), may hold values from -0.06629126 to 0.06629126
- fragment: int32 [4], replicated, may hold values from 0 to 3, each once
- anchor: float32 [8192, 1024], P('shard'), may hold values from -0.044194174 to 0.044194174
- momentum: float32 [8192, 1024], P('shard', 'rep'), may hold values from -0.078125 to 0.078125
Outputs:
- values: bfloat16 [32768, 1024], P(('rep', 'shard'))
- grad_tokens: bfloat16 [32768, 8192], P(('rep', 'shard'))
- grad_weight: bfloat16 [8, 8192, 1024], P('rep', 'shard')
- blended: bfloat16 [8, 8192, 1024], P('rep', 'shard')
- new_anchor: float32 [8192, 1024], P('shard')
- new_momentum: float32 [8192, 1024], P('shard', 'rep')
The draws below stay inside these ranges and needn't reach their ends.
All inputs are finite; a program needn't handle non-finite values.
Results may differ from the reference program's by a relative error of at most 0.00105.
Values may be sent and summed in bfloat16 or wider, within the bound.
No kernel may reach another device: no remote copies, remote signals or barrier semaphores. Data moves between devices by JAX's collectives and lax.ppermute only.
A program may use at most 192 MiB of HBM per device.

```python
import jax
import jax.numpy as jnp
from jax import lax

D = 8192
KV = 1024
LAYERS = 4
TOK_DEV = 256
TOKENS = 32768
N_REP = 8
N_SHARD = 16


def shared_anchor(key):
    return jax.random.truncated_normal(key, -4.0, 4.0, (D, KV), jnp.float32) * D ** (-0.5)


def draw_anchor(key, part):
    base = shared_anchor(key)
    return base


def draw_weights(key, part):
    base = shared_anchor(key)
    key = jax.random.fold_in(key, 23)
    drift = jax.random.truncated_normal(key, -4.0, 4.0, (N_REP, LAYERS, D, KV), jnp.float32)
    return (base[None, None] + 0.3 * D ** (-0.5) * drift).astype(jnp.bfloat16)


def block_levels(key, extent, cuts, smallest, largest):
    def one(position, blocks):
        draws = jax.random.uniform(jax.random.fold_in(jax.random.fold_in(key, 6), position), (blocks,), jnp.float32, smallest / len(cuts), largest / len(cuts))
        return jnp.repeat(jnp.exp(draws), extent[position] // blocks).reshape((-1,) + (1,) * (len(extent) - position - 1))

    factor_of = one(*cuts[0])
    for cut in cuts[1:]:
        factor_of = factor_of * one(*cut)
    return factor_of


def scatter_about(rng, extent, spread, most, split=(), kind=jnp.bfloat16):
    factor_of = block_levels(rng, extent, split, -0.22, 0.18) if split else 1.0
    entries = jax.random.normal(rng, extent, jnp.float32) * spread * factor_of
    return jnp.minimum(jnp.maximum(entries, -most), most).astype(kind)


def setup_inputs(seed: int = 0) -> dict:
    key_list = jax.random.split(jax.random.key(seed), 7)
    return {
        "tokens": scatter_about(key_list[0], (TOKENS, D), 1.0, 6.0, ((0, 128),)),
        "grad_values": scatter_about(key_list[1], (TOKENS, KV), 1.0, 6.0, ((0, 128),)),
        "weights": draw_weights(jax.random.fold_in(key_list[6], 71), 0),
        "fragment": jax.random.permutation(key_list[3], LAYERS).astype(jnp.int32),
        "anchor": draw_anchor(jax.random.fold_in(key_list[6], 71), 0),
        "momentum": scatter_about(key_list[5], (D, KV), (0.5 * D ** -0.5), 0.078125, ((0, 16), (1, 8)), jnp.float32),
    }


outer_momentum = 0.9
outer_rate = 0.7
mix_weight = 0.5


def replica_work(inputs):
    tok_block, cot_block, layer_weight = inputs
    flat_tok = tok_block.reshape(-1, tok_block.shape[-1])
    flat_cot = cot_block.reshape(-1, cot_block.shape[-1])
    values = jnp.dot(flat_tok, layer_weight, preferred_element_type=jnp.float32).astype(jnp.bfloat16)
    grad_tok = lax.dot_general(flat_cot, layer_weight, (((1,), (1,)), ((), ())), preferred_element_type=jnp.float32).astype(jnp.bfloat16)
    grad_sum = lax.dot_general(flat_tok, flat_cot, (((0,), (0,)), ((), ())), preferred_element_type=jnp.float32)
    return values, grad_tok, grad_sum.astype(jnp.bfloat16)


def reference(tokens, grad_values, weights, fragment, anchor, momentum):
    chosen = fragment[0].astype(jnp.int32)
    worked = fragment[1].astype(jnp.int32)
    synced = lax.dynamic_index_in_dim(weights, chosen, 1, keepdims=False)
    computed = lax.dynamic_index_in_dim(weights, worked, 1, keepdims=False)
    tok_blocks = tokens.reshape(N_REP, N_SHARD, TOK_DEV, D)
    cot_blocks = grad_values.reshape(N_REP, N_SHARD, TOK_DEV, KV)
    values, grad_tok, grad_weight = lax.map(replica_work, (tok_blocks, cot_blocks, computed))
    total = jnp.sum(synced.astype(jnp.float32), axis=0)
    outer_grad = anchor - total / N_REP
    new_momentum = outer_momentum * momentum + outer_grad
    new_anchor = anchor - outer_rate * (outer_grad + outer_momentum * new_momentum)
    blended = (mix_weight * synced.astype(jnp.float32) + (1.0 - mix_weight) * new_anchor[None]).astype(jnp.bfloat16)
    return (values.reshape(TOKENS, KV), grad_tok.reshape(TOKENS, D), grad_weight, blended, new_anchor, new_momentum)
```

```python
import jax
import jax.numpy as jnp
from jax import lax
from jax.experimental import pallas as pl
from jax.experimental.pallas import tpu as pltpu
from jax.sharding import PartitionSpec as P

outer_momentum = 0.9
outer_rate = 0.7
mix_weight = 0.5

NY = 4
BLOCK = 512
HALF = 256

RING = [(dy, dx) for dy in (0, 1, 3, 2) for dx in (0, 1)]


def y_shift(d):
    return [(s, ((s // 4 + d) % NY) * 4 + s % 4) for s in range(16)]


X_SWAP = [(s, s ^ 2) for s in range(16)]
CORE_SWAP = [(s, s ^ 1) for s in range(16)]


def send(x, pairs):
    return lax.ppermute(x, "shard", pairs)


def after(x, *deps):
    return lax.optimization_barrier((x, *deps))[0]


def wide_dot(a, b, dims):
    return lax.dot_general(a, b, (dims, ((), ())), preferred_element_type=jnp.float32)


def split_tokens(tokens, place):
    rows = tokens.shape[0]
    jobs = [(out, dx, cls, dy) for out, (dx, cls) in enumerate(((1, 1), (1, 0), (0, 1), (0, 0))) for dy in range(NY)]

    def body(place_ref, tok_ref, q1, p1, q0, p0, held, sems_in, sems_out):
        outs = (q1, p1, q0, p0)
        loads, stores = [], []
        for n, (out, dx, cls, dy) in enumerate(jobs):
            start = pl.multiple_of(place_ref[dy * 4 + dx * 2 + cls] * BLOCK, BLOCK)
            cp = pltpu.make_async_copy(tok_ref.at[:, pl.ds(start, BLOCK)], held.at[n], sems_in.at[n])
            cp.start()
            loads.append(cp)
        for n, (out, dx, cls, dy) in enumerate(jobs):
            loads[n].wait()
            cp = pltpu.make_async_copy(held.at[n], outs[out].at[dy], sems_out.at[n])
            cp.start()
            stores.append(cp)
        for cp in stores:
            cp.wait()

    return pl.pallas_call(
        body,
        out_shape=[jax.ShapeDtypeStruct((NY, rows, BLOCK), tokens.dtype)] * 4,
        in_specs=[pl.BlockSpec(memory_space=pltpu.SMEM), pl.BlockSpec(memory_space=pl.ANY)],
        out_specs=[pl.BlockSpec(memory_space=pl.ANY)] * 4,
        scratch_shapes=[
            pltpu.VMEM((len(jobs), rows, BLOCK), tokens.dtype),
            pltpu.SemaphoreType.DMA((len(jobs),)),
            pltpu.SemaphoreType.DMA((len(jobs),)),
        ],
        compiler_params=pltpu.CompilerParams(vmem_limit_bytes=16 * 2**20),
        cost_estimate=pl.CostEstimate(flops=0, bytes_accessed=2 * tokens.size * 2, transcendentals=0),
        name="split_tokens",
    )(place, tokens)


def place_columns(place, parts, width, into=None):
    rows = parts[0][0].shape[0]
    jobs = [(i, k, dy, dx, cls, h) for i, (_, cls, pieces) in enumerate(parts) for k, (dy, dx, h) in enumerate(pieces)]
    count = len(parts)

    def body(place_ref, *refs):
        srcs, (out, held, sems_in, sems_out) = refs[:count], refs[-4:]
        loads, stores = [], []
        for n, (i, k, dy, dx, cls, h) in enumerate(jobs):
            cp = pltpu.make_async_copy(srcs[i].at[:, pl.ds(k * HALF, HALF)], held.at[n], sems_in.at[n])
            cp.start()
            loads.append(cp)
        for n, (i, k, dy, dx, cls, h) in enumerate(jobs):
            loads[n].wait()
            start = pl.multiple_of(place_ref[dy * 4 + dx * 2 + cls] * BLOCK + h * HALF, HALF)
            cp = pltpu.make_async_copy(held.at[n], out.at[:, pl.ds(start, HALF)], sems_out.at[n])
            cp.start()
            stores.append(cp)
        for cp in stores:
            cp.wait()

    args = [place] + [p[0] for p in parts]
    specs = [pl.BlockSpec(memory_space=pltpu.SMEM)] + [pl.BlockSpec(memory_space=pl.ANY)] * count
    alias = {}
    if into is not None:
        args.append(into)
        specs.append(pl.BlockSpec(memory_space=pl.ANY))
        alias = {len(args) - 1: 0}
    dtype = parts[0][0].dtype
    return pl.pallas_call(
        body,
        out_shape=jax.ShapeDtypeStruct((rows, width), dtype),
        in_specs=specs,
        out_specs=pl.BlockSpec(memory_space=pl.ANY),
        scratch_shapes=[
            pltpu.VMEM((len(jobs), rows, HALF), dtype),
            pltpu.SemaphoreType.DMA((len(jobs),)),
            pltpu.SemaphoreType.DMA((len(jobs),)),
        ],
        input_output_aliases=alias,
        compiler_params=pltpu.CompilerParams(vmem_limit_bytes=16 * 2**20),
        cost_estimate=pl.CostEstimate(
            flops=0, bytes_accessed=2 * len(jobs) * rows * HALF * dtype.itemsize, transcendentals=0
        ),
        name="place_columns",
    )(*args)


def z_shift(d):
    return [(r, (r // 4) * 4 + (r + d) % 4) for r in range(8)]


def sum_over_rep(x, cols):
    x_lo, z = lax.axis_index("rep") // 4, lax.axis_index("rep") % 4
    half = 4 * cols
    away = lax.dynamic_slice_in_dim(x, (1 - x_lo) * half, half, 1)
    came = lax.ppermute(away, "rep", [(r, r ^ 4) for r in range(8)])
    pair = lax.dynamic_slice_in_dim(x, x_lo * half, half, 1).astype(jnp.float32) + came.astype(jnp.float32)

    def share(d):
        return lax.dynamic_slice_in_dim(pair, ((z + d) % 4) * cols, cols, 1)

    total = share(0)
    for d in (1, 3, 2):
        total = total + lax.ppermute(share(d), "rep", z_shift(d))
    return total


def local(tokens, grad_values, weights, fragment, anchor, momentum):
    me = lax.axis_index("shard")
    y, xh, core = me // 4, (me // 2) % 2, me % 2
    place = jnp.stack(
        [((y + dy) % NY) * 4 + (xh ^ dx) * 2 + (core ^ cls) for dy in range(NY) for dx in range(2) for cls in range(2)]
    ).astype(jnp.int32)

    layers = weights[0]
    synced = lax.dynamic_index_in_dim(layers, fragment[0], 0, keepdims=False)
    computed = lax.dynamic_index_in_dim(layers, fragment[1], 0, keepdims=False)
    w_a, w_b = computed[:HALF], computed[HALF:]

    synced_wide = synced.astype(jnp.float32)
    share_cols = momentum.shape[1]
    total = sum_over_rep(synced, share_cols)
    anchor_share = lax.dynamic_slice_in_dim(anchor, lax.axis_index("rep") * share_cols, share_cols, 1)
    outer_share = anchor_share - total / lax.axis_size("rep")
    new_momentum = outer_momentum * momentum + outer_share
    anchor_next = anchor_share - outer_rate * (outer_share + outer_momentum * new_momentum)
    new_anchor = lax.all_gather(anchor_next, "rep", axis=1, tiled=True)
    blended = (mix_weight * synced_wide + (1.0 - mix_weight) * new_anchor).astype(jnp.bfloat16)

    g_wb = jnp.concatenate([grad_values, w_b], 0)
    from_l = send(g_wb, y_shift(1))
    from_r = send(g_wb, y_shift(-1))
    w_x = send(computed, X_SWAP)

    q1, p1, q0, p0 = split_tokens(tokens, place)
    q1 = send(q1, CORE_SWAP)
    q0 = send(q0, CORE_SWAP)
    x1 = jnp.concatenate([p1, q1], 1)
    x0 = jnp.concatenate([p0, q0], 1)

    g_opp = send(from_l[:HALF], y_shift(1))
    wb_opp = send(from_r[HALF:], y_shift(-1))
    wb_lr = jnp.concatenate([from_r[HALF:], from_l[HALF:]], 0)
    wb_lr, w_x = lax.optimization_barrier((wb_lr, w_x))
    wb_lr_x = send(wb_lr, X_SWAP)
    wb_opp_x = send(after(wb_opp, wb_lr_x), X_SWAP)

    g_own = jnp.stack([grad_values, from_l[:HALF], from_r[:HALF], g_opp])
    g_oth = send(g_own, CORE_SWAP)
    g_line = jnp.concatenate([g_own, g_oth], 1)
    g_pair = g_line[0]
    g_all = g_line.reshape(-1, g_line.shape[-1])

    def exchange(x, *deps):
        a, b, d = x[1], x[3], x[2]
        if deps:
            a, b, d, *_ = lax.optimization_barrier((a, b, d, *deps))
        l = send(a, y_shift(1))
        r = send(b, y_shift(-1))
        o = send(d, y_shift(2))
        return jnp.concatenate([x[0], l, r, o], 0)

    line1 = exchange(x1, g_opp, wb_opp)
    part1 = wide_dot(line1, g_all, ((0,), (0,)))
    part1_x = send(part1, X_SWAP)
    line0 = exchange(x0, line1)
    part0 = wide_dot(line0, g_all, ((0,), (0,)))
    grad_weight = (part0 + part1_x).astype(jnp.bfloat16)

    wa_pair = jnp.concatenate([w_a, w_x[:HALF]], 0)
    wa_pair, line0 = lax.optimization_barrier((wa_pair, line0))
    wa_l = send(wa_pair, y_shift(1))
    wa_r = send(wa_pair, y_shift(-1))
    wa_opp0 = send(wa_l[:HALF], y_shift(1))
    wa_opp1 = send(wa_r[HALF:], y_shift(-1))

    x_of = (x0, x1)

    def piece(dy, dx, h):
        return x_of[dx][dy][:, h * HALF : (h + 1) * HALF]

    pieces_b = [(dy, dx, 1) for dy, dx in RING]
    pieces_a1 = [(dy, dx, 0) for dy, dx in RING[:6]]
    pieces_a2 = [(dy, dx, 0) for dy, dx in RING[6:]]
    rows = wb_lr_x.shape[0] // 2
    w_rows_b = jnp.concatenate(
        [w_b, w_x[HALF:], from_r[HALF:], wb_lr_x[:rows], from_l[HALF:], wb_lr_x[rows:], wb_opp, wb_opp_x], 0
    )
    w_rows_a1 = jnp.concatenate([wa_pair, wa_r, wa_l], 0)
    w_rows_a2 = jnp.concatenate([wa_opp0, wa_opp1], 0)

    def both(w_rows, pieces):
        x_cols = jnp.concatenate([piece(*p) for p in pieces], 1)
        v = wide_dot(x_cols, w_rows, ((1,), (0,)))
        gx = wide_dot(g_pair, w_rows, ((1,), (1,))).astype(jnp.bfloat16)
        mine, other = gx[:HALF], gx[HALF:]
        return v, [(mine, 0, pieces), (send(other, CORE_SWAP), 1, pieces)]

    v_b, gx_b = both(w_rows_b, pieces_b)
    v_a1, gx_a1 = both(w_rows_a1, pieces_a1)
    v_a2, gx_a2 = both(w_rows_a2, pieces_a2)
    v = (v_b + v_a1) + v_a2
    values = (v[:HALF] + send(v[HALF:], CORE_SWAP)).astype(jnp.bfloat16)
    token_grad = place_columns(place, gx_b + gx_a1, tokens.shape[1])
    token_grad = place_columns(place, gx_a2, tokens.shape[1], token_grad)

    return values, token_grad, grad_weight[None], blended[None], new_anchor, new_momentum


def solution(mesh):
    in_specs = (
        P(("rep", "shard"), None),
        P(("rep", "shard"), None),
        P("rep", None, "shard", None),
        P(),
        P("shard", None),
        P("shard", "rep"),
    )
    out_specs = (
        P(("rep", "shard"), None),
        P(("rep", "shard"), None),
        P("rep", "shard", None),
        P("rep", "shard", None),
        P("shard", None),
        P("shard", "rep"),
    )
    return jax.shard_map(local, mesh=mesh, in_specs=in_specs, out_specs=out_specs, check_vma=False)
```

```python
import jax
import jax.numpy as jnp
from jax import lax
from jax.experimental import pallas as pl
from jax.experimental.pallas import tpu as pltpu
from jax.sharding import PartitionSpec as P

outer_momentum = 0.9
outer_rate = 0.7
mix_weight = 0.5

NY = 4
VMEM = 60 * 2**20
BLOCK = 512
HALF = 256
SIDES = [(dx, dy) for dx in (1, 0) for dy in range(NY)]

X_SWAP = [(s, s ^ 2) for s in range(16)]
CORE_SWAP = [(s, s ^ 1) for s in range(16)]
LINES = [[y * 4 + k for y in range(NY)] for k in range(4)]
CHIP_LINES = [[y * 4 + xh * 2 + c for y in range(NY) for c in range(2)] for xh in range(2)]


def y_shift(d):
    return [(s, ((s // 4 + d) % NY) * 4 + s % 4) for s in range(16)]


def send(x, pairs):
    return lax.ppermute(x, "shard", pairs)


def z_shift(d):
    return [(r, (r // 4) * 4 + (r + d) % 4) for r in range(8)]


def rep_swap(x, bit):
    return lax.ppermute(x, "rep", [(r, r ^ bit) for r in range(8)])


def line_gather(x, groups):
    return lax.all_gather(x, "shard", axis=0, tiled=True, axis_index_groups=groups)


def wide_dot(a, b, dims):
    return lax.dot_general(a, b, (dims, ((), ())), preferred_element_type=jnp.float32)


class Spot:
    def __init__(self):
        me = lax.axis_index("shard")
        self.y, self.xh, self.core = me // 4, (me // 2) % 2, me % 2
        self.x_lo, self.z = lax.axis_index("rep") // 4, lax.axis_index("rep") % 4

    def row(self, dy):
        return (self.y + dy) % NY

    def columns(self, y, dx, cls, part=0, width=BLOCK):
        block = y * 4 + (self.xh ^ dx) * 2 + (self.core ^ cls)
        return pl.ds(pl.multiple_of(block * BLOCK + part, HALF), width)

    def tokens(self, cls):
        return pl.ds(pl.multiple_of((self.core ^ cls) * HALF, HALF), HALF)


def at(start, size):
    return pl.ds(pl.multiple_of(start, HALF), size)


def move(name, srcs, outs, plan, pick=None, keep=(), deps=()):
    srcs, outs, keep, deps = list(srcs), list(outs), list(keep), list(deps)
    n_pick = 0 if pick is None else 1
    n_in = n_pick + len(srcs) + len(keep) + len(deps)
    n_out = len(outs) + len(keep)
    shapes, n_stores = [], 0
    if plan is not None:

        class Origin:
            y = xh = core = x_lo = z = 0
            row = lambda self, dy: dy
            columns = lambda self, *a: None
            tokens = lambda self, c: None

        draft = plan(Origin(), [0] * 4)
        shapes = [(job[2], srcs[job[0]].dtype) for job in draft]
        n_stores = sum(len(job[3]) for job in draft)

    def body(*refs):
        if plan is None:
            return
        src_refs = refs[n_pick : n_pick + len(srcs)]
        out_refs = refs[n_in : n_in + n_out]
        held, (sems_in, sems_out) = refs[n_in + n_out : -2], refs[-2:]
        jobs = plan(Spot(), refs[0] if n_pick else None)
        loads, stores = [], []
        for n, (i, index, _, _) in enumerate(jobs):
            cp = pltpu.make_async_copy(src_refs[i].at[index], held[n], sems_in.at[n])
            cp.start()
            loads.append(cp)
        for n, (_, _, _, writes) in enumerate(jobs):
            loads[n].wait()
            for j, index, part in writes:
                src = held[n] if part is None else held[n].at[part]
                cp = pltpu.make_async_copy(src, out_refs[j].at[index], sems_out.at[len(stores)])
                cp.start()
                stores.append(cp)
        for cp in stores:
            cp.wait()

    anywhere = pl.BlockSpec(memory_space=pl.ANY)
    scratch = [pltpu.VMEM(shape, dtype) for shape, dtype in shapes]
    if shapes:
        scratch += [pltpu.SemaphoreType.DMA((len(shapes),)), pltpu.SemaphoreType.DMA((n_stores,))]
    args = ([] if pick is None else [pick]) + srcs + keep + deps
    return list(
        pl.pallas_call(
            body,
            out_shape=[jax.ShapeDtypeStruct(o.shape, o.dtype) for o in outs + keep],
            in_specs=[pl.BlockSpec(memory_space=pltpu.SMEM)] * n_pick + [anywhere] * (n_in - n_pick),
            out_specs=[anywhere] * n_out,
            scratch_shapes=scratch,
            input_output_aliases={n_pick + len(srcs) + k: len(outs) + k for k in range(len(keep))},
            compiler_params=pltpu.CompilerParams(vmem_limit_bytes=VMEM),
            cost_estimate=pl.CostEstimate(flops=1, bytes_accessed=1, transcendentals=0),
            name=name,
        )(*args)
    )


def bf16(*shape):
    return jax.ShapeDtypeStruct(shape, jnp.bfloat16)


def place_columns(parts, width, into=None):
    rows = parts[0][0].shape[0]
    srcs = [p[0] for p in parts]
    last = 0

    def plan(spot, _):
        jobs = []
        for i, (_, cls, pieces) in enumerate(parts):
            for k, (y, dx, h) in enumerate(pieces):
                cut = (pl.ds(0, rows), pl.ds(k * HALF, HALF))
                put = (pl.ds(0, rows), spot.columns(y, dx, cls, h * HALF, HALF))
                jobs.append((i, cut, (rows, HALF), [(last, put, None)]))
        return jobs

    outs, keep = ([bf16(rows, width)], []) if into is None else ([], [into])
    return move("place_columns", srcs, outs, plan, keep=keep)[0]


def split_half(total, here):
    width = total.shape[1] // 2
    cut = lambda k: lax.dynamic_slice_in_dim(total, k * width, width, 1)
    return cut(here), cut(1 - here)


def local(tokens, grad_values, weights, fragment, anchor, momentum):
    me, rep = lax.axis_index("shard"), lax.axis_index("rep")
    y, core = me // 4, me % 2
    x_lo, z_hi, z_lo = rep // 4, (rep // 2) % 2, rep % 2
    cols = grad_values.shape[1]
    rows = tokens.shape[0]
    top, low = pl.ds(0, HALF), pl.ds(HALF, HALF)
    every, half = pl.ds(0, BLOCK), (HALF, cols)

    wb, wa = move(
        "pick_rows",
        [weights],
        [bf16(*half), bf16(*half)],
        lambda spot, f: [(0, (0, f[1], low), half, [(0, (top,), None)]), (0, (0, f[1], top), half, [(1, (top,), None)])],
        pick=fragment,
    )
    wb_line = line_gather(wb, LINES)
    wa_x = send(wa, X_SWAP)

    def split(spot, f):
        jobs = [
            (0, (top, spot.columns(spot.row(dy), dx, 1)), (rows, BLOCK), [(0, (n,), None)])
            for n, (dx, dy) in enumerate(SIDES)
        ]
        jobs.append((1, (top,), half, [(1, (top,), None)]))
        side = (1 - spot.x_lo) * (cols // 2)
        jobs.append((2, (0, f[0], every, at(side, cols // 2)), (BLOCK, cols // 2), [(2, (every,), None)]))
        for n, (dx, dy) in enumerate(SIDES):
            writes = [(3 + n, (spot.tokens(0),), None)] + spread(spot, dx, dy, top, 11)
            jobs.append((0, (top, spot.columns(spot.row(dy), dx, 0)), (rows, BLOCK), writes))
        return jobs

    def spread(spot, dx, dy, where, first):
        yy = spot.row(dy)
        return [
            (first + dx, (where, at(yy * HALF, HALF)), (top, low)),
            (first + 2, (where, at(yy * BLOCK + dx * HALF, HALF)), (top, top)),
        ]

    x_other, g_own, away, *x_parts = move(
        "split_tokens",
        [tokens, grad_values, weights],
        [bf16(8, rows, BLOCK), bf16(*half), bf16(BLOCK, cols // 2)]
        + [bf16(BLOCK, BLOCK)] * 8
        + [bf16(BLOCK, NY * HALF)] * 2
        + [bf16(BLOCK, NY * BLOCK)],
        split,
        pick=fragment,
        deps=[wb],
    )
    x_other = send(x_other, CORE_SWAP)
    g_line = line_gather(g_own, CHIP_LINES)
    came = rep_swap(away, 4)

    def fill(spot, _):
        return [
            (0, (n,), (rows, BLOCK), [(n, (spot.tokens(1),), None)] + spread(spot, dx, dy, low, 8))
            for n, (dx, dy) in enumerate(SIDES)
        ]

    x_parts = move("fill_tokens", [x_other], [], fill, keep=x_parts)
    s1, s0, x_b, x_a = x_parts[:4], x_parts[4:8], x_parts[8:10], x_parts[10]

    l1, r1, o1 = send(s1[1], y_shift(1)), send(s1[3], y_shift(-1)), send(s1[2], y_shift(2))

    wa_pair, wb_line, came = move(
        "a_pair",
        [wa, wa_x],
        [bf16(BLOCK, cols)],
        lambda *_: [(0, (top,), half, [(0, (top,), None)]), (1, (top,), half, [(0, (low,), None)])],
        keep=[wb_line, came],
        deps=[l1, r1],
    )
    wb_line_x = send(wb_line, X_SWAP)
    wa_line = line_gather(wa_pair, LINES)

    synced = lax.dynamic_index_in_dim(weights[0], fragment[0], 0, keepdims=False)
    share_cols = momentum.shape[1]

    mine = lax.dynamic_slice_in_dim(synced, x_lo * (cols // 2), cols // 2, 1).astype(jnp.float32)
    total = mine + came.astype(jnp.float32)
    total, away = split_half(total, z_hi)
    came = rep_swap(away, 2)

    line = tuple(enumerate((0, -1, 1, 2)))
    line1_top, line1_low, s0[1], s0[3], came = move(
        "line_across",
        [s1[0], l1, r1, o1],
        [bf16(NY * BLOCK, HALF)] * 2,
        lambda spot, _: [
            (
                n,
                (every,),
                (BLOCK, BLOCK),
                [(h, (at(spot.row(dy) * BLOCK, BLOCK),), (every, cut)) for h, cut in enumerate((top, low))],
            )
            for n, dy in line
        ],
        keep=[s0[1], s0[3], came],
    )
    l0, r0 = send(s0[1], y_shift(1)), send(s0[3], y_shift(-1))
    total, away = split_half(total + came, z_lo)
    total = total + rep_swap(away, 1)
    anchor_share = lax.dynamic_slice_in_dim(anchor, rep * share_cols, share_cols, 1)
    outer_share = anchor_share - total / lax.axis_size("rep")
    new_momentum = outer_momentum * momentum + outer_share
    found = anchor_share - outer_rate * (outer_share + outer_momentum * new_momentum)
    came = rep_swap(found, 4)

    part1_top = wide_dot(line1_top, g_line, ((0,), (0,)))
    part1_top_x = send(part1_top, X_SWAP)
    part1_low = wide_dot(line1_low, g_line, ((0,), (0,)))

    f32 = lambda count: jax.ShapeDtypeStruct((BLOCK, count * share_cols), jnp.float32)
    blocks = lambda k, count=1: (every, pl.ds(pl.multiple_of(k * share_cols, share_cols), count * share_cols))

    def beside(count, here):
        def plan(spot, _):
            mine = here(spot)
            return [
                (i, (every,), (BLOCK, count * share_cols), [(0, blocks(k * count, count), None)])
                for i, k in enumerate((mine, 1 - mine))
            ]

        return plan

    x_b = move("after_part", [], [], None, keep=x_b, deps=[part1_top, part1_low])

    (s0[2],) = move("last_cols", [], [], None, keep=[s0[2]], deps=[l0, r0, part1_top, part1_low])
    o0 = send(s0[2], y_shift(2))
    g_beside = lax.dynamic_slice_in_dim(g_line, y * BLOCK + (1 - core) * HALF, HALF, 0)
    g_pair = jnp.concatenate([grad_values, g_beside], 0)

    def both(x_part, w_rows, pieces):
        v = wide_dot(x_part, w_rows, ((1,), (0,)))
        gx = wide_dot(g_pair, w_rows, ((1,), (1,))).astype(jnp.bfloat16)
        return v, [(gx[:HALF], 0, pieces), (send(gx[HALF:], CORE_SWAP), 1, pieces)]

    v_b0, gx_b0 = both(x_b[0], wb_line, [(yy, 0, 1) for yy in range(NY)])

    v_b1, gx_b1 = both(x_b[1], wb_line_x, [(yy, 1, 1) for yy in range(NY)])
    v_b = v_b0 + v_b1

    found, part1_low = move(
        "last_part",
        [found, came],
        [f32(2)],
        beside(1, lambda spot: spot.x_lo),
        keep=[part1_low],
        deps=[part1_top_x, o0, v_b, gx_b0[0][0], gx_b1[0][0]],
    )
    part1_low_x = send(part1_low, X_SWAP)
    shares = [found] + [lax.ppermute(found, "rep", z_shift(d)) for d in (1, -1, 2)]

    v_a, gx_a = both(x_a, wa_line, [(yy, dx, 0) for yy in range(NY) for dx in range(2)])
    v = v_b + v_a

    def anchor_columns(spot, _):
        return [
            (i, blocks(xx), (BLOCK, share_cols), [(0, blocks(xx * 4 + (spot.z + dz) % 4), None)])
            for i, dz in enumerate((0, 3, 1, 2))
            for xx in range(2)
        ]

    (new_anchor,) = move("anchor_columns", shares, [f32(8)], anchor_columns)
    blended = (mix_weight * synced.astype(jnp.float32) + (1.0 - mix_weight) * new_anchor).astype(jnp.bfloat16)

    values = (v[:HALF] + send(v[HALF:], CORE_SWAP)).astype(jnp.bfloat16)
    token_grad = place_columns(gx_b0 + gx_b1, tokens.shape[1])
    token_grad = place_columns(gx_a, tokens.shape[1], token_grad)

    (line0,) = move(
        "line_own",
        [s0[0], l0, r0, o0],
        [bf16(NY * BLOCK, BLOCK)],
        lambda spot, _: [
            (n, (every,), (BLOCK, BLOCK), [(0, (at(spot.row(dy) * BLOCK, BLOCK),), None)]) for n, dy in line
        ],
        deps=[part1_low],
    )
    part0 = wide_dot(line0, g_line, ((0,), (0,)))
    (part1_low_x,) = move("rest", [], [], None, keep=[part1_low_x], deps=[part0, new_anchor])
    grad_weight = (part0 + jnp.concatenate([part1_top_x, part1_low_x], 0)).astype(jnp.bfloat16)

    return values, token_grad, grad_weight[None], blended[None], new_anchor, new_momentum


def solution(mesh):
    in_specs = (
        P(("rep", "shard"), None),
        P(("rep", "shard"), None),
        P("rep", None, "shard", None),
        P(),
        P("shard", None),
        P("shard", "rep"),
    )
    out_specs = (
        P(("rep", "shard"), None),
        P(("rep", "shard"), None),
        P("rep", "shard", None),
        P("rep", "shard", None),
        P("shard", None),
        P("shard", "rep"),
    )
    return jax.shard_map(local, mesh=mesh, in_specs=in_specs, out_specs=out_specs, check_vma=False)
```

```python
import jax
import jax.numpy as jnp
from jax import lax
from jax.experimental import pallas as pl
from jax.experimental.pallas import tpu as pltpu
from jax.sharding import PartitionSpec as P

outer_momentum = 0.9
outer_rate = 0.7
mix_weight = 0.5

NY = 4
VMEM = 60 * 2**20
BLOCK = 512
HALF = 256
SIDES = [(dx, dy) for dx in (1, 0) for dy in range(NY)]

X_SWAP = [(s, s ^ 2) for s in range(16)]
CORE_SWAP = [(s, s ^ 1) for s in range(16)]
LINES = [[y * 4 + k for y in range(NY)] for k in range(4)]
CHIP_LINES = [[y * 4 + xh * 2 + c for y in range(NY) for c in range(2)] for xh in range(2)]


def y_shift(d):
    return [(s, ((s // 4 + d) % NY) * 4 + s % 4) for s in range(16)]


def send(x, pairs):
    return lax.ppermute(x, "shard", pairs)


def z_shift(d):
    return [(r, (r // 4) * 4 + (r + d) % 4) for r in range(8)]


def rep_swap(x, bit):
    return lax.ppermute(x, "rep", [(r, r ^ bit) for r in range(8)])


def line_gather(x, groups):
    return lax.all_gather(x, "shard", axis=0, tiled=True, axis_index_groups=groups)


def wide_dot(a, b, dims):
    return lax.dot_general(a, b, (dims, ((), ())), preferred_element_type=jnp.float32)


class Spot:
    def __init__(self):
        me = lax.axis_index("shard")
        self.y, self.xh, self.core = me // 4, (me // 2) % 2, me % 2
        self.x_lo, self.z = lax.axis_index("rep") // 4, lax.axis_index("rep") % 4

    def row(self, dy):
        return (self.y + dy) % NY

    def columns(self, y, dx, cls, part=0, width=BLOCK):
        block = y * 4 + (self.xh ^ dx) * 2 + (self.core ^ cls)
        return pl.ds(pl.multiple_of(block * BLOCK + part, HALF), width)

    def tokens(self, cls):
        return pl.ds(pl.multiple_of((self.core ^ cls) * HALF, HALF), HALF)


def at(start, size):
    return pl.ds(pl.multiple_of(start, HALF), size)


def move(name, srcs, outs, plan, pick=None, keep=(), deps=()):
    srcs, outs, keep, deps = list(srcs), list(outs), list(keep), list(deps)
    n_pick = 0 if pick is None else 1
    n_in = n_pick + len(srcs) + len(keep) + len(deps)
    n_out = len(outs) + len(keep)
    shapes, n_stores = [], 0
    if plan is not None:

        class Origin:
            y = xh = core = x_lo = z = 0
            row = lambda self, dy: dy
            columns = lambda self, *a: None
            tokens = lambda self, c: None

        draft = plan(Origin(), [0] * 4)
        shapes = [(job[2], srcs[job[0]].dtype) for job in draft]
        n_stores = sum(len(job[3]) for job in draft)

    def body(*refs):
        if plan is None:
            return
        src_refs = refs[n_pick : n_pick + len(srcs)]
        out_refs = refs[n_in : n_in + n_out]
        held, (sems_in, sems_out) = refs[n_in + n_out : -2], refs[-2:]
        jobs = plan(Spot(), refs[0] if n_pick else None)
        loads, stores = [], []
        for n, (i, index, _, _) in enumerate(jobs):
            cp = pltpu.make_async_copy(src_refs[i].at[index], held[n], sems_in.at[n])
            cp.start()
            loads.append(cp)
        for n, (_, _, _, writes) in enumerate(jobs):
            loads[n].wait()
            for j, index, part in writes:
                src = held[n] if part is None else held[n].at[part]
                cp = pltpu.make_async_copy(src, out_refs[j].at[index], sems_out.at[len(stores)])
                cp.start()
                stores.append(cp)
        for cp in stores:
            cp.wait()

    anywhere = pl.BlockSpec(memory_space=pl.ANY)
    scratch = [pltpu.VMEM(shape, dtype) for shape, dtype in shapes]
    if shapes:
        scratch += [pltpu.SemaphoreType.DMA((len(shapes),)), pltpu.SemaphoreType.DMA((n_stores,))]
    args = ([] if pick is None else [pick]) + srcs + keep + deps
    return list(
        pl.pallas_call(
            body,
            out_shape=[jax.ShapeDtypeStruct(o.shape, o.dtype) for o in outs + keep],
            in_specs=[pl.BlockSpec(memory_space=pltpu.SMEM)] * n_pick + [anywhere] * (n_in - n_pick),
            out_specs=[anywhere] * n_out,
            scratch_shapes=scratch,
            input_output_aliases={n_pick + len(srcs) + k: len(outs) + k for k in range(len(keep))},
            compiler_params=pltpu.CompilerParams(vmem_limit_bytes=VMEM),
            cost_estimate=pl.CostEstimate(flops=1, bytes_accessed=1, transcendentals=0),
            name=name,
        )(*args)
    )


def bf16(*shape):
    return jax.ShapeDtypeStruct(shape, jnp.bfloat16)


def place_columns(parts, width, into=None, deps=()):
    rows = parts[0][0].shape[0]
    srcs = [p[0] for p in parts]
    last = 0

    def plan(spot, _):
        jobs = []
        for i, (_, cls, pieces) in enumerate(parts):
            for k, (y, dx, h) in enumerate(pieces):
                cut = (pl.ds(0, rows), pl.ds(k * HALF, HALF))
                put = (pl.ds(0, rows), spot.columns(y, dx, cls, h * HALF, HALF))
                jobs.append((i, cut, (rows, HALF), [(last, put, None)]))
        return jobs

    outs, keep = ([bf16(rows, width)], []) if into is None else ([], [into])
    return move("place_columns", srcs, outs, plan, keep=keep, deps=deps)[0]


def split_half(total, here):
    width = total.shape[1] // 2
    cut = lambda k: lax.dynamic_slice_in_dim(total, k * width, width, 1)
    return cut(here), cut(1 - here)


def local(tokens, grad_values, weights, fragment, anchor, momentum):
    me, rep = lax.axis_index("shard"), lax.axis_index("rep")
    y, core = me // 4, me % 2
    x_lo, z_hi, z_lo = rep // 4, (rep // 2) % 2, rep % 2
    cols = grad_values.shape[1]
    rows = tokens.shape[0]
    top, low = pl.ds(0, HALF), pl.ds(HALF, HALF)
    every, half = pl.ds(0, BLOCK), (HALF, cols)

    wb, wa = move(
        "pick_rows",
        [weights],
        [bf16(*half), bf16(*half)],
        lambda spot, f: [(0, (0, f[1], low), half, [(0, (top,), None)]), (0, (0, f[1], top), half, [(1, (top,), None)])],
        pick=fragment,
    )
    wb_line = line_gather(wb, LINES)
    wa_x = send(wa, X_SWAP)

    def split(spot, f):
        jobs = [
            (0, (top, spot.columns(spot.row(dy), dx, 1)), (rows, BLOCK), [(0, (n,), None)])
            for n, (dx, dy) in enumerate(SIDES)
        ]
        jobs.append((1, (top,), half, [(1, (top,), None)]))
        side = (1 - spot.x_lo) * (cols // 2)
        jobs.append((2, (0, f[0], every, at(side, cols // 2)), (BLOCK, cols // 2), [(2, (every,), None)]))
        for n, (dx, dy) in enumerate(SIDES):
            writes = [(3 + n, (spot.tokens(0),), None)] + spread(spot, dx, dy, top, 11)
            jobs.append((0, (top, spot.columns(spot.row(dy), dx, 0)), (rows, BLOCK), writes))
        return jobs

    def spread(spot, dx, dy, where, first):
        yy = spot.row(dy)
        return [
            (first + dx, (where, at(yy * HALF, HALF)), (top, low)),
            (first + 2, (where, at(yy * BLOCK + dx * HALF, HALF)), (top, top)),
        ]

    x_other, g_own, away, *x_parts = move(
        "split_tokens",
        [tokens, grad_values, weights],
        [bf16(8, rows, BLOCK), bf16(*half), bf16(BLOCK, cols // 2)]
        + [bf16(BLOCK, BLOCK)] * 8
        + [bf16(BLOCK, NY * HALF)] * 2
        + [bf16(BLOCK, NY * BLOCK)],
        split,
        pick=fragment,
        deps=[wb],
    )
    x_other = send(x_other, CORE_SWAP)
    g_line = line_gather(g_own, CHIP_LINES)
    came = rep_swap(away, 4)

    def fill(spot, _):
        return [
            (0, (n,), (rows, BLOCK), [(n, (spot.tokens(1),), None)] + spread(spot, dx, dy, low, 8))
            for n, (dx, dy) in enumerate(SIDES)
        ]

    x_parts = move("fill_tokens", [x_other], [], fill, keep=x_parts)
    s1, s0, x_b, x_a = x_parts[:4], x_parts[4:8], x_parts[8:10], x_parts[10]

    l1, r1, o1 = send(s1[1], y_shift(1)), send(s1[3], y_shift(-1)), send(s1[2], y_shift(2))

    upper, lower = pl.ds(0, BLOCK), pl.ds(BLOCK, BLOCK)
    wa_pair, wb_upper, wb_lower, came = move(
        "a_pair",
        [wa, wa_x, wb_line],
        [bf16(BLOCK, cols)] * 3,
        lambda *_: [
            (2, (upper,), (BLOCK, cols), [(1, (every,), None)]),
            (2, (lower,), (BLOCK, cols), [(2, (every,), None)]),
            (0, (top,), half, [(0, (top,), None)]),
            (1, (top,), half, [(0, (low,), None)]),
        ],
        keep=[came],
        deps=[l1, r1],
    )
    wb_upper_x = send(wb_upper, X_SWAP)
    wa_line = line_gather(wa_pair, LINES)

    synced = lax.dynamic_index_in_dim(weights[0], fragment[0], 0, keepdims=False)
    share_cols = momentum.shape[1]

    mine = lax.dynamic_slice_in_dim(synced, x_lo * (cols // 2), cols // 2, 1).astype(jnp.float32)
    total = mine + came.astype(jnp.float32)
    total, away = split_half(total, z_hi)
    came = rep_swap(away, 2)

    line = tuple(enumerate((0, -1, 1, 2)))
    line1_top, line1_low, s0[1], s0[3], came, wb_lower = move(
        "line_across",
        [s1[0], l1, r1, o1],
        [bf16(NY * BLOCK, HALF)] * 2,
        lambda spot, _: [
            (
                n,
                (every,),
                (BLOCK, BLOCK),
                [(h, (at(spot.row(dy) * BLOCK, BLOCK),), (every, cut)) for h, cut in enumerate((top, low))],
            )
            for n, dy in line
        ],
        keep=[s0[1], s0[3], came, wb_lower],
        deps=[wb_upper_x],
    )
    wb_lower_x = send(wb_lower, X_SWAP)
    l0, r0 = send(s0[1], y_shift(1)), send(s0[3], y_shift(-1))
    total, away = split_half(total + came, z_lo)
    total = total + rep_swap(away, 1)
    anchor_share = lax.dynamic_slice_in_dim(anchor, rep * share_cols, share_cols, 1)
    outer_share = anchor_share - total / lax.axis_size("rep")
    new_momentum = outer_momentum * momentum + outer_share
    found = anchor_share - outer_rate * (outer_share + outer_momentum * new_momentum)
    came = rep_swap(found, 4)

    part1_top = wide_dot(line1_top, g_line, ((0,), (0,)))
    part1_top_x = send(part1_top, X_SWAP)
    part1_low = wide_dot(line1_low, g_line, ((0,), (0,)))

    f32 = lambda count: jax.ShapeDtypeStruct((BLOCK, count * share_cols), jnp.float32)
    blocks = lambda k, count=1: (every, pl.ds(pl.multiple_of(k * share_cols, share_cols), count * share_cols))

    def beside(count, here):
        def plan(spot, _):
            mine = here(spot)
            return [
                (i, (every,), (BLOCK, count * share_cols), [(0, blocks(k * count, count), None)])
                for i, k in enumerate((mine, 1 - mine))
            ]

        return plan

    (s0[2],) = move("last_cols", [], [], None, keep=[s0[2]], deps=[l0, r0, part1_top, part1_low])
    o0 = send(s0[2], y_shift(2))
    wb_line_x, *x_b = move(
        "after_part",
        [wb_upper_x, wb_lower_x],
        [bf16(2 * BLOCK, cols)],
        lambda *_: [(i, (every,), (BLOCK, cols), [(0, (cut,), None)]) for i, cut in enumerate((upper, lower))],
        keep=x_b,
        deps=[part1_top, part1_low, s0[2]],
    )

    g_beside = lax.dynamic_slice_in_dim(g_line, y * BLOCK + (1 - core) * HALF, HALF, 0)
    g_pair = jnp.concatenate([grad_values, g_beside], 0)

    def both(x_part, w_rows, pieces):
        v = wide_dot(x_part, w_rows, ((1,), (0,)))
        gx = wide_dot(g_pair, w_rows, ((1,), (1,))).astype(jnp.bfloat16)
        return v, [(gx[:HALF], 0, pieces), (send(gx[HALF:], CORE_SWAP), 1, pieces)]

    v_b0, gx_b0 = both(x_b[0], wb_line, [(yy, 0, 1) for yy in range(NY)])

    v_b1, gx_b1 = both(x_b[1], wb_line_x, [(yy, 1, 1) for yy in range(NY)])
    v_b = v_b0 + v_b1

    (line0,) = move(
        "line_own",
        [s0[0], l0, r0, o0],
        [bf16(NY * BLOCK, BLOCK)],
        lambda spot, _: [
            (n, (every,), (BLOCK, BLOCK), [(0, (at(spot.row(dy) * BLOCK, BLOCK),), None)]) for n, dy in line
        ],
        deps=[v_b],
    )
    part0 = wide_dot(line0, g_line, ((0,), (0,)))

    found, part1_low = move(
        "last_part",
        [found, came],
        [f32(2)],
        beside(1, lambda spot: spot.x_lo),
        keep=[part1_low],
        deps=[part1_top_x, part0, gx_b0[0][0], gx_b1[0][0]],
    )
    part1_low_x = send(part1_low, X_SWAP)
    shares = [found] + [lax.ppermute(found, "rep", z_shift(d)) for d in (1, -1, 2)]

    (wa_line,) = move("a_line", [], [], None, keep=[wa_line], deps=[part1_low])
    pieces_a = [(yy, dx, 0) for yy in range(NY) for dx in range(2)]

    def a_products(rows_of):
        gx = wide_dot(g_pair[rows_of], wa_line, ((1,), (1,))).astype(jnp.bfloat16)
        return gx, v_b[rows_of] + wide_dot(x_a[rows_of], wa_line, ((1,), (0,)))

    gx_other, v_other = a_products(slice(HALF, None))
    gx_other, v_other = send(gx_other, CORE_SWAP), send(v_other, CORE_SWAP)
    gx_mine, v_mine = a_products(slice(0, HALF))
    gx_a = [(gx_mine, 0, pieces_a), (gx_other, 1, pieces_a)]

    def anchor_columns(spot, _):
        return [
            (i, blocks(xx), (BLOCK, share_cols), [(0, blocks(xx * 4 + (spot.z + dz) % 4), None)])
            for i, dz in enumerate((0, 3, 1, 2))
            for xx in range(2)
        ]

    (new_anchor,) = move("anchor_columns", shares, [f32(8)], anchor_columns, deps=[gx_mine, v_mine])
    blended = (mix_weight * synced.astype(jnp.float32) + (1.0 - mix_weight) * new_anchor).astype(jnp.bfloat16)

    values = (v_mine + v_other).astype(jnp.bfloat16)
    token_grad = place_columns(gx_b0 + gx_b1, tokens.shape[1], deps=[part1_low])
    token_grad = place_columns(gx_a, tokens.shape[1], token_grad)

    (part1_low_x,) = move("rest", [], [], None, keep=[part1_low_x], deps=[part0, new_anchor])
    grad_weight = (part0 + jnp.concatenate([part1_top_x, part1_low_x], 0)).astype(jnp.bfloat16)

    return values, token_grad, grad_weight[None], blended[None], new_anchor, new_momentum


def solution(mesh):
    in_specs = (
        P(("rep", "shard"), None),
        P(("rep", "shard"), None),
        P("rep", None, "shard", None),
        P(),
        P("shard", None),
        P("shard", "rep"),
    )
    out_specs = (
        P(("rep", "shard"), None),
        P(("rep", "shard"), None),
        P("rep", "shard", None),
        P("rep", "shard", None),
        P("shard", None),
        P("shard", "rep"),
    )
    return jax.shard_map(local, mesh=mesh, in_specs=in_specs, out_specs=out_specs, check_vma=False)
```
